32 devices in a mesh: gz: 16 (over z, y, core), gy: 2 (over x).
Axes of the slice: x: 2, y: 2, z: 4, core: 2. Of those that a mesh axis runs over, the one named last changes fastest.
Arguments:
- density: float32 [160, 32, 2048], P('gz', 'gy'), may hold values from -6 to 6
- dilations: int32 [3], replicated, may hold values from 1 to 4, as said below
- owner_rank: int32 [8192, 1], P(('gz', 'gy')), may hold values from 0 to 1; in each aligned block of 256 rows (0 to 255, 256 to 511, ...) at most 128 rows name the same one
- owner_slot: int32 [8192], P(('gz', 'gy')), may hold values from 0 to 255
- base_cell: int32 [8192], P(('gz', 'gy')), may hold values from 0 to 276479
- corner_weights: float32 [8, 8192], P(None, ('gz', 'gy')), may hold values from 0.05 to 1
Outputs:
- response: float32 [160, 32, 2048], P('gz', 'gy')
- catalogue: float32 [3, 8192], P(None, ('gz', 'gy'))
The draws below stay inside these ranges and needn't reach their ends.
Inputs may be any that keep to these rules, and one draw needn't show every extreme that they name: `dilations`: one level has dilation 4 and another has dilation 1. `owner_rank`: the entries listed on one device name one owner at most 128 times; some owner is named exactly 128 times by some device.
All inputs are finite; a program needn't handle non-finite values.
Results may differ from the reference program's by a relative error of at most 0.00014.
Values sent between devices are 32-bit elements; how exact they have to be, the bound alone decides.
A program may use at most 192 MiB of HBM per device.

```python
import math
import jax
import jax.numpy as jnp
import numpy as np

SCALES = 3
DMAX = 4
CZ = 10
CY = 16
NX = 2048
NZ = 160
NY = 32
HSLOT = 256
CAP = 128
HOWN = 256
SLOTS = 8192
N_GZ = 16
N_GY = 2


def draw_dilations(key, part):
    key_values, key_pick = jax.random.split(key)
    spacing = jax.random.randint(key_values, (SCALES,), 1, DMAX + 1)
    chosen = jax.random.randint(key_pick, (), 0, SCALES)
    levels = jnp.arange(SCALES)
    spacing = jnp.where(levels == chosen, DMAX, spacing)
    spacing = jnp.where(levels == (chosen + 1) % SCALES, 1, spacing)
    return spacing.astype(jnp.int32)


def set_ends(drawn, rng, least, top_value):
    spot = [jax.random.randint(jax.random.fold_in(rng, axis), (), 0, length) for axis, length in enumerate(drawn.shape)]
    widest = drawn.shape.index(max(drawn.shape))
    next_to = spot[:widest] + [(spot[widest] + 1) % drawn.shape[widest]] + spot[widest + 1:]
    return drawn.at[tuple(spot)].set(least).at[tuple(next_to)].set(top_value)


def level_of(rng, dims, cuts, low, largest):
    def one(axis_at, parts):
        steps = jax.random.uniform(jax.random.fold_in(jax.random.fold_in(rng, 6), axis_at), (parts,), jnp.float32, low / len(cuts), largest / len(cuts))
        return jnp.repeat(jnp.exp(steps), dims[axis_at] // parts).reshape((-1,) + (1,) * (len(dims) - axis_at - 1))

    loudness = one(*cuts[0])
    for cut in cuts[1:]:
        loudness = loudness * one(*cut)
    return loudness


def routed_block(rng, own, number, rows, number_of, top, limit, slope):
    order = jax.random.permutation(rng, number_of)
    packed, common = shares(number_of, rows * top, limit, slope, True), shares(number_of, rows * top, limit, slope, False)
    places = jnp.arange(number_of)

    def named(lengths, rotation):
        used = int((lengths > 0).sum())
        fixed = max(1, used // 4)
        moved = fixed + (places - fixed + rotation * (used - fixed)) % max(1, number_of - fixed)
        return jnp.zeros((number_of,), jnp.int32).at[order[jnp.where(places < fixed, places, moved)]].set(jnp.asarray(lengths, jnp.int32))

    lengths = jnp.where(number % 4 == 0, named(packed, number // 4), named(common, number - number // 4 - 1))
    mixed = jax.random.permutation(jax.random.fold_in(own, 3), number_of)
    giver, sink = mixed[0:number_of // 2 * 2:2], mixed[1:number_of // 2 * 2:2]
    room = jnp.minimum(lengths[giver] - 1, limit - lengths[sink]) // 2
    room = jnp.where((giver == order[0]) | (sink == order[0]) | (lengths[sink] == 0), 0, jnp.maximum(room, 0))
    moved = jax.random.randint(jax.random.fold_in(own, 4), (number_of // 2,), 0, 1 << 20) % (room + 1)
    lengths = lengths.at[giver].add(-moved).at[sink].add(moved)
    items = jnp.searchsorted(jnp.cumsum(lengths), jnp.arange(rows * top), side="right").astype(jnp.int32)
    listing = items.reshape(top, rows).T
    listing = listing[jax.random.permutation(jax.random.fold_in(own, 1), rows)]
    rotation = jax.random.randint(jax.random.fold_in(own, 2), (rows, 1), 0, top)
    return jnp.take_along_axis(listing, (jnp.arange(top)[None, :] + rotation) % top, axis=1)


def shares(number_of, total, bound, lean, full):
    portions = [(1 << 20) // math.isqrt(grade ** lean) + 1 for grade in range(1, number_of + 1)]
    largest = bound if full else min(bound, max(-(-total // number_of), total * portions[0] // sum(portions)))
    least = 1 if total - largest >= number_of - 1 else 0
    holding, surplus = [largest] + [least] * (number_of - 1), total - largest - least * (number_of - 1)
    while surplus > 0:
        movable = [i for i in range(1, number_of) if holding[i] < largest] or [i for i in range(1, number_of) if holding[i] < bound]
        whole, budget = sum([portions[i] for i in movable]), surplus
        for i in movable:
            addition = min(bound - holding[i], max(1, budget * portions[i] // whole), surplus)
            holding[i] = holding[i] + addition
            surplus = surplus - addition
    return np.array(holding)


def noise(own_key, dims, deviation, reach, pieces=(), held_as=jnp.bfloat16):
    gain = level_of(own_key, dims, pieces, -0.22, 0.18) if pieces else 1.0
    drawn = jax.random.normal(own_key, dims, jnp.float32) * deviation * gain
    return jnp.minimum(jnp.maximum(drawn, -reach), reach).astype(held_as)


def setup_inputs(seed: int = 0) -> dict:
    arg_keys = jax.random.split(jax.random.key(seed), 7)
    density = noise(arg_keys[0], (NZ, NY, NX), 1.0, 6.0, ((0, 16), (1, 2)), jnp.float32)
    dilations = draw_dilations(jax.random.fold_in(arg_keys[6], 71), 0)
    owner_rank_keys = jax.random.split(jax.random.fold_in(arg_keys[2], 1), SLOTS // HSLOT)
    owner_rank_turns = jax.random.permutation(jax.random.fold_in(arg_keys[2], 3), SLOTS // HSLOT)
    owner_rank = jax.vmap(lambda own, number: routed_block(jax.random.fold_in(arg_keys[2], 2), own, number, HSLOT, N_GY, 1, CAP, 2))(owner_rank_keys, owner_rank_turns).reshape((SLOTS, 1))
    owner_slot = set_ends(jax.random.randint(arg_keys[3], (SLOTS,), 0, HOWN), jax.random.fold_in(arg_keys[3], 1), 0, HOWN - 1).astype(jnp.int32)
    base_cell = set_ends(jax.random.randint(arg_keys[4], (SLOTS,), 0, (CZ - 1) * (CY - 1) * NX), jax.random.fold_in(arg_keys[4], 1), 0, ((CZ - 1) * (CY - 1) * NX) - 1).astype(jnp.int32)
    corner_weights = jnp.clip(0.05 + 0.95 * jax.random.uniform(arg_keys[5], (8, SLOTS), jnp.float32) ** level_of(arg_keys[5], (8, SLOTS), ((1, 32),), -0.2, 0.2), 0.05, 1.0)
    return {"density": density, "dilations": dilations, "owner_rank": owner_rank, "owner_slot": owner_slot, "base_cell": base_cell, "corner_weights": corner_weights}


tap_weights = (0.0625, 0.25, 0.375, 0.25, 0.0625)
hessian_scale = 4.0


def smooth_cycle(field_data, dilation, along_dim):
    running = None
    for offset in range(5):
        summand = tap_weights[offset] * jnp.roll(field_data, -(offset - 2) * dilation, axis=along_dim)
        running = summand if running is None else running + summand
    return running


def invariants(curve_zz, curve_yy, curve_xx, curve_zy, curve_zx, curve_yx):
    trace_sum = curve_xx + curve_yy + curve_zz
    minor_sum = curve_xx * curve_yy + curve_xx * curve_zz + curve_yy * curve_zz - curve_zy * curve_zy - curve_zx * curve_zx - curve_yx * curve_yx
    return (trace_sum * trace_sum / 3.0 - minor_sum) * jax.nn.sigmoid(-trace_sum)


def signature(smoothed):
    centre = smoothed
    above_z = jnp.roll(smoothed, -1, 0)
    below_z = jnp.roll(smoothed, 1, 0)
    above_y = jnp.roll(smoothed, -1, 1)
    below_y = jnp.roll(smoothed, 1, 1)
    curve_zz = hessian_scale * (above_z - 2.0 * centre + below_z)
    curve_yy = hessian_scale * (above_y - 2.0 * centre + below_y)
    curve_xx = hessian_scale * (jnp.roll(centre, -1, 2) - 2.0 * centre + jnp.roll(centre, 1, 2))
    curve_zy = hessian_scale * 0.25 * (jnp.roll(above_z, -1, 1) - jnp.roll(above_z, 1, 1) - jnp.roll(below_z, -1, 1) + jnp.roll(below_z, 1, 1))
    curve_zx = hessian_scale * 0.25 * (jnp.roll(above_z, -1, 2) - jnp.roll(above_z, 1, 2) - jnp.roll(below_z, -1, 2) + jnp.roll(below_z, 1, 2))
    curve_yx = hessian_scale * 0.25 * (jnp.roll(above_y, -1, 2) - jnp.roll(above_y, 1, 2) - jnp.roll(below_y, -1, 2) + jnp.roll(below_y, 1, 2))
    return invariants(curve_zz, curve_yy, curve_xx, curve_zy, curve_zx, curve_yx)


def reference(density, dilations, owner_rank, owner_slot, base_cell, corner_weights):
    response = None
    levels = []
    for level_index in range(SCALES):
        dilation = dilations[level_index]
        smoothed = smooth_cycle(density, dilation, 1)
        smoothed = smooth_cycle(smoothed, dilation, 0)
        smoothed = smooth_cycle(smoothed, dilation, 2)
        feature = signature(smoothed)
        response = feature if response is None else jnp.maximum(response, feature)
        levels.append(feature)
    feature_table = jnp.stack(levels)
    slot_rows = jnp.arange(SLOTS, dtype=jnp.int32)
    device = slot_rows // HSLOT
    z_group = device // N_GY
    y_group = device % N_GY
    plane = (CY - 1) * NX
    z_index = base_cell // plane
    remainder = base_cell % plane
    y_index = remainder // NX
    x_index = remainder % NX
    partial_value = None
    corner = 0
    for step_z in (0, 1):
        for step_y in (0, 1):
            for step_x in (0, 1):
                picked = feature_table[:, z_group * CZ + z_index + step_z, y_group * CY + y_index + step_y, (x_index + step_x) % NX]
                summand = corner_weights[corner] * picked
                partial_value = summand if partial_value is None else partial_value + summand
                corner += 1
    column = z_group * (N_GY * HOWN) + owner_rank[:, 0] * HOWN + owner_slot
    catalogue = jnp.zeros((SCALES, N_GZ * N_GY * HOWN), jnp.float32).at[:, column].add(partial_value)
    return response, catalogue
```

```python
import functools

import jax
import jax.numpy as jnp
from jax import lax
from jax.experimental import pallas as pl
from jax.experimental.pallas import tpu as pltpu
from jax.sharding import PartitionSpec as P

SCALES = 3
HALO = 9
HOWN = 256
DMAX = 4
LANES = 128
TAPS = (0.375, 0.25, 0.0625)


def taps(centre, near, far, scale=1.0):
    return (TAPS[0] * scale) * centre + (TAPS[1] * scale) * near + (TAPS[2] * scale) * far


def kernel(depth, rows, width, bands, *refs):
    dil_ref, select_ref, xcell_ref, column_ref = refs[:4]
    parts = refs[4 : 4 + 3 * bands]
    resp_ref, cat_ref, field, along, smooth, feature, sems = refs[4 + 3 * bands :]
    tiles = width // LANES
    starts = (0, HALO, HALO + depth)
    copies = []
    for b in range(bands):
        for i in range(3):
            src = parts[3 * b + i]
            copies.append(
                pltpu.make_async_copy(
                    src,
                    field.at[pl.ds(starts[i], src.shape[0]), pl.ds(b * rows, rows)],
                    sems.at[3 * b + i],
                )
            )
    for copy in copies:
        copy.start()
    resp_ref[...] = jnp.full(resp_ref.shape, -jnp.inf, jnp.float32)
    for copy in copies:
        copy.wait()

    places = ((rows,), (0, 2 * rows)) if bands == 2 else ((rows,), (0,), (2 * rows,))
    lane = lax.broadcasted_iota(jnp.int32, (8, LANES), 1)
    groups = (rows + 2 + 7) // 8

    def level_body(level, carry):
        d = dil_ref[level]
        d2 = 2 * d

        def z_body(p, c):
            at = p + HALO - 1
            for b in range(bands):
                for r in range(0, rows, 8):
                    for x in range(0, width, 512):
                        def plane(k):
                            return field[at + k, b * rows + r : b * rows + r + 8, x : x + 512]

                        v = taps(plane(0), plane(d) + plane(-d), plane(d2) + plane(-d2))
                        for place in places[b]:
                            along[p, place + r : place + r + 8, x : x + 512] = v
            return c

        lax.fori_loop(0, depth + 2, z_body, 0)

        def xy_pass(d):
            d2 = 2 * d
            up1, up2 = lane < LANES - d, lane < LANES - d2
            dn1, dn2 = lane >= d, lane >= d2

            def xy_body(p, c):
                for g in range(groups):
                    base = rows - 1 + 8 * g

                    def row(k, j):
                        return along[p, base + k : base + k + 8, j * LANES : (j + 1) * LANES]

                    def prepare(j):
                        t = taps(row(0, j), row(d, j) + row(-d, j), row(d2, j) + row(-d2, j))
                        return (t,) + tuple(
                            pltpu.roll(t, shift, 1) for shift in (LANES - d, LANES - d2, d, d2)
                        )

                    ready = {j: prepare(j) for j in (tiles - 1, 0)}
                    for j in range(tiles):
                        n, m = (j + 1) % tiles, (j - 1) % tiles
                        if n not in ready:
                            ready[n] = prepare(n)
                        t, l1, l2, r1, r2 = ready[j]
                        near = jnp.where(up1, l1, ready[n][1]) + jnp.where(dn1, r1, ready[m][3])
                        far = jnp.where(up2, l2, ready[n][2]) + jnp.where(dn2, r2, ready[m][4])
                        smooth[p, 8 * g : 8 * g + 8, j * LANES : (j + 1) * LANES] = taps(
                            t, near, far, 4.0
                        )
                return c

            lax.fori_loop(0, depth + 2, xy_body, 0)

        for spacing in range(1, DMAX + 1):
            pl.when(d == spacing)(functools.partial(xy_pass, spacing))

        first, last = lane == 0, lane == LANES - 1

        def hess_body(z, c):
            for r in range(0, rows, 8):
                def at(dz, dy, j):
                    return smooth[
                        z + 1 + dz, r + 1 + dy : r + 9 + dy, j * LANES : (j + 1) * LANES
                    ]

                def prepare(j):
                    centre, zp, zm = at(0, 0, j), at(1, 0, j), at(-1, 0, j)
                    yp, ym = at(0, 1, j), at(0, -1, j)
                    twice = centre + centre
                    hzz = (zp + zm) - twice
                    hyy = (yp + ym) - twice
                    zy = (at(1, 1, j) - at(1, -1, j)) - (at(-1, 1, j) - at(-1, -1, j))
                    shifted = [
                        (pltpu.roll(v, LANES - 1, 1), pltpu.roll(v, 1, 1))
                        for v in (centre, zp - zm, yp - ym)
                    ]
                    return twice, hzz, hyy, zy, shifted

                def finish(j, low, mid, high):
                    twice, hzz, hyy, zy, shifted = mid
                    plus = [jnp.where(last, high[4][i][0], shifted[i][0]) for i in range(3)]
                    minus = [jnp.where(first, low[4][i][1], shifted[i][1]) for i in range(3)]
                    hxx = (plus[0] + minus[0]) - twice
                    zx = plus[1] - minus[1]
                    yx = plus[2] - minus[2]
                    flat = hxx + hyy
                    trace = flat + hzz
                    squares = 0.0625 * (zy * zy + zx * zx + yx * yx)
                    minors = hxx * hyy + flat * hzz - squares
                    value = (trace * trace * (1.0 / 3.0) - minors) / (1.0 + jnp.exp(trace))
                    lanes = slice(j * LANES, (j + 1) * LANES)
                    resp_ref[z, r : r + 8, lanes] = jnp.maximum(resp_ref[z, r : r + 8, lanes], value)
                    feature[pl.ds(pl.multiple_of(z * rows + r, 8), 8), lanes] = value

                ready = {j: prepare(j) for j in (tiles - 1, 0)}
                for j in range(tiles):
                    n = (j + 1) % tiles
                    if n not in ready:
                        ready[n] = prepare(n)
                    finish(j, ready[(j - 1) % tiles], ready[j], ready[n])
            return c

        lax.fori_loop(0, depth, hess_body, 0)

        xcell = xcell_ref[...]
        slots = xcell.shape[0]
        chunk = 512

        def gather_body(i, acc):
            x0 = pl.multiple_of(i * chunk, chunk)
            block = feature[:, pl.ds(x0, chunk)]
            where = lax.broadcasted_iota(jnp.int32, (slots, chunk), 1) + x0
            for dx in range(2):
                cell = xcell + dx
                cell = jnp.where(cell == width, 0, cell)
                picked = jnp.dot(
                    select_ref[dx],
                    block,
                    precision=lax.Precision.HIGHEST,
                    preferred_element_type=jnp.float32,
                )
                acc = acc + jnp.sum(jnp.where(where == cell, picked, 0.0), axis=1, keepdims=True)
            return acc

        partial = lax.fori_loop(0, width // chunk, gather_body, jnp.zeros((slots, 1), jnp.float32))
        column = lax.broadcasted_iota(jnp.int32, (slots, cat_ref.shape[2]), 1)
        spread = jnp.where(column == column_ref[...], partial, 0.0)
        cat_ref[level] = jnp.sum(spread, axis=0, keepdims=True)
        return carry

    lax.fori_loop(0, SCALES, level_body, 0)


def ring(axis, step):
    count = lax.axis_size(axis)
    return [(i, (i + step) % count) for i in range(count)]


def per_device(density, dilations, owner_rank, owner_slot, base_cell, corner_weights):
    depth, rows, width = density.shape
    groups = lax.axis_size("gy")

    def z_sides(block):
        low = lax.ppermute(block[depth - HALO :], "gz", ring("gz", 1))
        high = lax.ppermute(block[:HALO], "gz", ring("gz", -1))
        return [low, block, high]

    parts = z_sides(density)
    neighbours = [lax.ppermute(density, "gy", ring("gy", 1))]
    if groups != 2:
        neighbours.append(lax.ppermute(density, "gy", ring("gy", -1)))
    for band in neighbours:
        parts += z_sides(band)
    bands = 1 + len(neighbours)

    plane = (rows - 1) * width
    z_index = base_cell // plane
    remainder = base_cell % plane
    y_index = remainder // width
    x_index = remainder % width
    row_at = jnp.arange(depth * rows, dtype=jnp.int32)[None, :]
    select = []
    for step_x in (0, 1):
        chosen = 0.0
        for step_z in (0, 1):
            for step_y in (0, 1):
                row = (z_index + step_z) * rows + y_index + step_y
                weight = corner_weights[4 * step_z + 2 * step_y + step_x]
                chosen = chosen + jnp.where(row[:, None] == row_at, weight[:, None], 0.0)
        select.append(chosen)
    select = jnp.stack(select)
    column = owner_rank * HOWN + owner_slot[:, None]

    vmem = pl.BlockSpec(memory_space=pltpu.VMEM)
    cells = depth * rows * width
    response, spread = pl.pallas_call(
        functools.partial(kernel, depth, rows, width, bands),
        out_shape=(
            jax.ShapeDtypeStruct((depth, rows, width), jnp.float32),
            jax.ShapeDtypeStruct((SCALES, 1, groups * HOWN), jnp.float32),
        ),
        in_specs=[pl.BlockSpec(memory_space=pltpu.SMEM), vmem, vmem, vmem]
        + [pl.BlockSpec(memory_space=pl.ANY)] * (3 * bands),
        out_specs=(vmem, vmem),
        scratch_shapes=[
            pltpu.VMEM((depth + 2 * HALO, bands * rows, width), jnp.float32),
            pltpu.VMEM((depth + 2, 3 * rows, width), jnp.float32),
            pltpu.VMEM((depth + 2, (rows + 2 + 7) // 8 * 8, width), jnp.float32),
            pltpu.VMEM((depth * rows, width), jnp.float32),
            pltpu.SemaphoreType.DMA((3 * bands,)),
        ],
        compiler_params=pltpu.CompilerParams(vmem_limit_bytes=56 * 1024 * 1024),
        cost_estimate=pl.CostEstimate(
            flops=cells * SCALES * 100, bytes_accessed=cells * 4 * 8, transcendentals=cells * SCALES
        ),
    )(dilations, select, x_index[:, None], column, *parts)

    spread = spread[:, 0]
    me = lax.axis_index("gy")

    def share(owner):
        return lax.dynamic_slice_in_dim(spread, owner * HOWN, HOWN, axis=1)

    catalogue = share(me)
    for step in range(1, groups):
        catalogue = catalogue + lax.ppermute(
            share((me + step) % groups), "gy", ring("gy", step)
        )
    return (response, catalogue)


def solution(mesh):
    placed = (
        P("gz", "gy", None),
        P(),
        P(("gz", "gy"), None),
        P(("gz", "gy")),
        P(("gz", "gy")),
        P(None, ("gz", "gy")),
    )
    return jax.shard_map(
        per_device,
        mesh=mesh,
        in_specs=placed,
        out_specs=(P("gz", "gy", None), P(None, ("gz", "gy"))),
        check_vma=False,
    )
```

```python
import functools

import jax
import jax.numpy as jnp
from jax import lax
from jax.experimental import pallas as pl
from jax.experimental.pallas import tpu as pltpu
from jax.sharding import PartitionSpec as P

SCALES = 3
HALO = 9
HOWN = 256
DMAX = 4
LANES = 128
TAPS = (0.375, 0.25, 0.0625)


def taps(centre, near, far, scale=1.0):
    return (TAPS[0] * scale) * centre + (TAPS[1] * scale) * near + (TAPS[2] * scale) * far


def kernel(depth, rows, bands, tiles, first_tile, width, pieces, aliased, *refs):
    dil_ref, select_ref, xcell_ref, column_ref = refs[:4]
    count = 4 + 3 * bands * len(pieces)
    parts = refs[4:count]
    if aliased:
        count += 1
    out_ref, cat_ref, field, along, smooth, feature, chosen, resp, sems = refs[count:]
    span = tiles * LANES
    kept = span - 2 * LANES
    starts = (0, HALO, HALO + depth)
    copies = []
    for n, (low, size, to) in enumerate(pieces):
        for b in range(bands):
            for i in range(3):
                src = parts[(n * bands + b) * 3 + i]
                planes = depth if i == 1 else HALO
                copies.append(
                    pltpu.make_async_copy(
                        src.at[:, :, pl.ds(low[src.shape[2] == width], size)],
                        field.at[pl.ds(starts[i], planes), pl.ds(b * rows, rows), pl.ds(to, size)],
                        sems.at[len(copies)],
                    )
                )
    for copy in copies:
        copy.start()
    resp[...] = jnp.full(resp.shape, -jnp.inf, jnp.float32)
    for dx in range(2):
        weights = select_ref[dx]
        high = weights.astype(jnp.bfloat16)
        rest = (weights - high.astype(jnp.float32)).astype(jnp.bfloat16)
        chosen[dx] = jnp.concatenate([high, high, rest], axis=1)
    for copy in copies:
        copy.wait()

    places = ((rows,), (0, 2 * rows)) if bands == 2 else ((rows,), (0,), (2 * rows,))
    lane = lax.broadcasted_iota(jnp.int32, (8, LANES), 1)
    groups = (rows + 2 + 7) // 8

    def level_body(level, carry):
        d = dil_ref[level]
        d2 = 2 * d

        def z_body(p, c):
            at = p + HALO - 1
            for b in range(bands):
                for r in range(0, rows, 8):
                    for x in range(0, span, 512):
                        def plane(k):
                            return field[at + k, b * rows + r : b * rows + r + 8, x : x + 512]

                        v = taps(plane(0), plane(d) + plane(-d), plane(d2) + plane(-d2))
                        for place in places[b]:
                            along[p, place + r : place + r + 8, x : x + 512] = v
            return c

        lax.fori_loop(0, depth + 2, z_body, 0)

        def xy_pass(d):
            d2 = 2 * d
            up1, up2 = lane < LANES - d, lane < LANES - d2
            dn1, dn2 = lane >= d, lane >= d2

            def xy_body(p, c):
                for g in range(groups):
                    base = rows - 1 + 8 * g

                    def row(k, j):
                        return along[p, base + k : base + k + 8, j * LANES : (j + 1) * LANES]

                    def prepare(j):
                        t = taps(row(0, j), row(d, j) + row(-d, j), row(d2, j) + row(-d2, j))
                        return (t,) + tuple(
                            pltpu.roll(t, shift, 1) for shift in (LANES - d, LANES - d2, d, d2)
                        )

                    ready = {j: prepare(j) for j in (tiles - 1, 0)}
                    for j in range(tiles):
                        n, m = (j + 1) % tiles, (j - 1) % tiles
                        if n not in ready:
                            ready[n] = prepare(n)
                        t, l1, l2, r1, r2 = ready[j]
                        near = jnp.where(up1, l1, ready[n][1]) + jnp.where(dn1, r1, ready[m][3])
                        far = jnp.where(up2, l2, ready[n][2]) + jnp.where(dn2, r2, ready[m][4])
                        smooth[p, 8 * g : 8 * g + 8, j * LANES : (j + 1) * LANES] = taps(
                            t, near, far, 4.0
                        )
                return c

            lax.fori_loop(0, depth + 2, xy_body, 0)

        for spacing in range(1, DMAX + 1):
            pl.when(d == spacing)(functools.partial(xy_pass, spacing))

        first, last = lane == 0, lane == LANES - 1

        def hess_body(z, c):
            for r in range(0, rows, 8):
                def at(dz, dy, j):
                    return smooth[
                        z + 1 + dz, r + 1 + dy : r + 9 + dy, j * LANES : (j + 1) * LANES
                    ]

                def prepare(j):
                    centre, zp, zm = at(0, 0, j), at(1, 0, j), at(-1, 0, j)
                    yp, ym = at(0, 1, j), at(0, -1, j)
                    twice = centre + centre
                    hzz = (zp + zm) - twice
                    hyy = (yp + ym) - twice
                    zy = (at(1, 1, j) - at(1, -1, j)) - (at(-1, 1, j) - at(-1, -1, j))
                    shifted = [
                        (pltpu.roll(v, LANES - 1, 1), pltpu.roll(v, 1, 1))
                        for v in (centre, zp - zm, yp - ym)
                    ]
                    return twice, hzz, hyy, zy, shifted

                def finish(j, low, mid, high):
                    twice, hzz, hyy, zy, shifted = mid
                    plus = [jnp.where(last, high[4][i][0], shifted[i][0]) for i in range(3)]
                    minus = [jnp.where(first, low[4][i][1], shifted[i][1]) for i in range(3)]
                    hxx = (plus[0] + minus[0]) - twice
                    zx = plus[1] - minus[1]
                    yx = plus[2] - minus[2]
                    flat = hxx + hyy
                    trace = flat + hzz
                    squares = 0.0625 * (zy * zy + zx * zx + yx * yx)
                    minors = hxx * hyy + flat * hzz - squares
                    value = (trace * trace * (1.0 / 3.0) - minors) / (1.0 + jnp.exp(trace))
                    lanes = slice((j - 1) * LANES, j * LANES)
                    resp[z, r : r + 8, lanes] = jnp.maximum(resp[z, r : r + 8, lanes], value)
                    feature[pl.ds(pl.multiple_of(z * rows + r, 8), 8), lanes] = value

                ready = [prepare(0), prepare(1)]
                for j in range(1, tiles - 1):
                    ready.append(prepare(j + 1))
                    finish(j, *ready[j - 1 : j + 2])
            return c

        lax.fori_loop(0, depth, hess_body, 0)

        xcell = xcell_ref[...]
        slots = xcell.shape[0]
        chunk = 256

        def gather_body(i, acc):
            x0 = pl.multiple_of(i * chunk, chunk)
            block = feature[:, pl.ds(x0, chunk)]
            high = block.astype(jnp.bfloat16)
            rest = (block - high.astype(jnp.float32)).astype(jnp.bfloat16)
            block = jnp.concatenate([high, rest, high], axis=0)
            where = lax.broadcasted_iota(jnp.int32, (slots, chunk), 1) + x0
            where = where + (first_tile + 1) * LANES
            where = jnp.where(where >= width, where - width, where)
            for dx in range(2):
                cell = xcell + dx
                cell = jnp.where(cell == width, 0, cell)
                picked = jnp.dot(chosen[dx], block, preferred_element_type=jnp.float32)
                acc = acc + jnp.sum(jnp.where(where == cell, picked, 0.0), axis=1, keepdims=True)
            return acc

        partial = lax.fori_loop(0, kept // chunk, gather_body, jnp.zeros((slots, 1), jnp.float32))
        column = lax.broadcasted_iota(jnp.int32, (slots, cat_ref.shape[2]), 1)
        spread = jnp.where(column == column_ref[...], partial, 0.0)
        cat_ref[level] = jnp.sum(spread, axis=0, keepdims=True)
        return carry

    lax.fori_loop(0, SCALES, level_body, 0)

    until = min(kept, width - (first_tile + 1) * LANES)
    outs = [(0, (first_tile + 1) * LANES, until)]
    if until < kept:
        outs.append((until, 0, kept - until))
    copies = [
        pltpu.make_async_copy(
            resp.at[:, :, pl.ds(low, size)], out_ref.at[:, :, pl.ds(to, size)], sems.at[n]
        )
        for n, (low, to, size) in enumerate(outs)
    ]
    for copy in copies:
        copy.start()
    for copy in copies:
        copy.wait()


def ring(axis, step):
    count = lax.axis_size(axis)
    return [(i, (i + step) % count) for i in range(count)]


def per_device(density, dilations, owner_rank, owner_slot, base_cell, corner_weights):
    depth, rows, width = density.shape
    groups = lax.axis_size("gy")

    half = width // 2

    def z_sides(block):
        low = lax.ppermute(block[depth - HALO :], "gz", ring("gz", 1))
        high = lax.ppermute(block[:HALO], "gz", ring("gz", -1))
        return low, high

    def y_sides(block):
        sides = [lax.ppermute(block, "gy", ring("gy", 1))]
        if groups != 2:
            sides.append(lax.ppermute(block, "gy", ring("gy", -1)))
        return sides

    front = density[:, :, :half]
    beside = y_sides(front)
    low, high = z_sides(front)
    beside, later = lax.optimization_barrier((beside, density))
    parts_a = [low, density, high]
    back = later[:, :, half:]
    beside_b = y_sides(back)
    for band in beside:
        low, high = z_sides(band)
        parts_a += [low, band, high]
    low, high = z_sides(back)
    parts_b = [low, density, high]
    beside_b, parts_a = lax.optimization_barrier((beside_b, parts_a))
    for band in beside_b:
        low, high = z_sides(band)
        parts_b += [low, band, high]
    bands = 1 + len(beside)

    plane = (rows - 1) * width
    z_index = base_cell // plane
    remainder = base_cell % plane
    y_index = remainder // width
    x_index = remainder % width
    row_at = jnp.arange(depth * rows, dtype=jnp.int32)[None, :]
    select = []
    for step_x in (0, 1):
        chosen = 0.0
        for step_z in (0, 1):
            for step_y in (0, 1):
                row = (z_index + step_z) * rows + y_index + step_y
                weight = corner_weights[4 * step_z + 2 * step_y + step_x]
                chosen = chosen + jnp.where(row[:, None] == row_at, weight[:, None], 0.0)
        select.append(chosen)
    select = jnp.stack(select)
    column = owner_rank * HOWN + owner_slot[:, None]

    vmem = pl.BlockSpec(memory_space=pltpu.VMEM)
    anywhere = pl.BlockSpec(memory_space=pl.ANY)
    half_tiles = half // LANES

    def run(tiles, first_tile, pieces, parts, onto):
        cells = depth * rows * tiles * LANES
        operands = [dilations, select, x_index[:, None], column] + parts
        in_specs = [pl.BlockSpec(memory_space=pltpu.SMEM), vmem, vmem, vmem]
        in_specs += [anywhere] * len(parts)
        aliases = {}
        if onto is not None:
            aliases = {len(operands): 0}
            operands.append(onto)
            in_specs.append(anywhere)
        return pl.pallas_call(
            functools.partial(
                kernel, depth, rows, bands, tiles, first_tile, width, pieces, onto is not None
            ),
            out_shape=(
                jax.ShapeDtypeStruct((depth, rows, width), jnp.float32),
                jax.ShapeDtypeStruct((SCALES, 1, groups * HOWN), jnp.float32),
            ),
            in_specs=in_specs,
            out_specs=(anywhere, vmem),
            input_output_aliases=aliases,
            scratch_shapes=[
                pltpu.VMEM((depth + 2 * HALO, bands * rows, tiles * LANES), jnp.float32),
                pltpu.VMEM((depth + 2, 3 * rows, tiles * LANES), jnp.float32),
                pltpu.VMEM((depth + 2, (rows + 2 + 7) // 8 * 8, tiles * LANES), jnp.float32),
                pltpu.VMEM((depth * rows, (tiles - 2) * LANES), jnp.float32),
                pltpu.VMEM((2, base_cell.shape[0], 3 * depth * rows), jnp.bfloat16),
                pltpu.VMEM((depth, rows, (tiles - 2) * LANES), jnp.float32),
                pltpu.SemaphoreType.DMA((len(parts),)),
            ],
            compiler_params=pltpu.CompilerParams(vmem_limit_bytes=48 * 1024 * 1024),
            cost_estimate=pl.CostEstimate(
                flops=cells * SCALES * 100,
                bytes_accessed=cells * 4 * 8,
                transcendentals=cells * SCALES,
            ),
        )(*operands)

    edge = 2 * LANES
    pieces_a = (((0, 0), half, 0),)
    pieces_b = (
        ((half - edge, half - edge), edge, 0),
        ((0, half), half, edge),
        ((0, 0), edge, edge + half),
    )
    response, spread_a = run(half_tiles, 0, pieces_a, parts_a, None)
    response, spread_b = run(
        half_tiles + 4, half_tiles - 2, pieces_b, parts_a + parts_b + parts_a, response
    )
    spread = spread_a + spread_b

    spread = spread[:, 0]
    me = lax.axis_index("gy")

    def share(owner):
        return lax.dynamic_slice_in_dim(spread, owner * HOWN, HOWN, axis=1)

    catalogue = share(me)
    for step in range(1, groups):
        catalogue = catalogue + lax.ppermute(
            share((me + step) % groups), "gy", ring("gy", step)
        )
    return (response, catalogue)


def solution(mesh):
    placed = (
        P("gz", "gy", None),
        P(),
        P(("gz", "gy"), None),
        P(("gz", "gy")),
        P(("gz", "gy")),
        P(None, ("gz", "gy")),
    )
    return jax.shard_map(
        per_device,
        mesh=mesh,
        in_specs=placed,
        out_specs=(P("gz", "gy", None), P(None, ("gz", "gy"))),
        check_vma=False,
    )
```

```python
import functools

import jax
import jax.numpy as jnp
from jax import lax
from jax.experimental import pallas as pl
from jax.experimental.pallas import tpu as pltpu
from jax.sharding import PartitionSpec as P

SCALES = 3
HALO = 9
HOWN = 256
DMAX = 4
LANES = 128
TAPS = (0.375, 0.25, 0.0625)


def taps(centre, near, far, scale=1.0):
    return (TAPS[0] * scale) * centre + (TAPS[1] * scale) * near + (TAPS[2] * scale) * far


def kernel(depth, rows, bands, tiles, first_tile, width, pieces, aliased, *refs):
    dil_ref, select_ref, xcell_ref, column_ref = refs[:4]
    count = 4 + 3 * bands * len(pieces)
    parts = refs[4:count]
    if aliased:
        count += 1
    out_ref, cat_ref, field, along, smooth, feature, chosen, resp, sems = refs[count:]
    span = tiles * LANES
    kept = span - 2 * LANES
    starts = (0, HALO, HALO + depth)
    copies = []
    for n, (low, size, to) in enumerate(pieces):
        for b in range(bands):
            for i in range(3):
                src = parts[(n * bands + b) * 3 + i]
                planes = depth if i == 1 else HALO
                copies.append(
                    pltpu.make_async_copy(
                        src.at[:, :, pl.ds(low[src.shape[2] == width], size)],
                        field.at[pl.ds(starts[i], planes), pl.ds(b * rows, rows), pl.ds(to, size)],
                        sems.at[len(copies)],
                    )
                )
    for copy in copies:
        copy.start()
    resp[...] = jnp.full(resp.shape, -jnp.inf, jnp.float32)
    for dx in range(2):
        weights = select_ref[dx]
        high = weights.astype(jnp.bfloat16)
        rest = (weights - high.astype(jnp.float32)).astype(jnp.bfloat16)
        chosen[dx] = jnp.concatenate([high, high, rest], axis=1)
    for copy in copies:
        copy.wait()

    places = ((rows,), (0, 2 * rows)) if bands == 2 else ((rows,), (0,), (2 * rows,))
    lane = lax.broadcasted_iota(jnp.int32, (8, LANES), 1)
    groups = rows // 8
    sub = lax.broadcasted_iota(jnp.int32, (8, LANES), 0)
    top, bottom = sub == 0, sub == 7

    def level_body(level, carry):
        d = dil_ref[level]
        d2 = 2 * d

        def z_body(p, c):
            at = p + HALO - 1
            for b in range(bands):
                for r in range(0, rows, 8):
                    for x in range(0, span, 512):
                        def plane(k):
                            return field[at + k, b * rows + r : b * rows + r + 8, x : x + 512]

                        v = taps(plane(0), plane(d) + plane(-d), plane(d2) + plane(-d2))
                        for place in places[b]:
                            along[p, place + r : place + r + 8, x : x + 512] = v
            return c

        lax.fori_loop(0, depth + 2, z_body, 0)

        def xy_pass(d):
            d2 = 2 * d
            up1, up2 = lane < LANES - d, lane < LANES - d2
            dn1, dn2 = lane >= d, lane >= d2

            def xy_body(p, c):
                for g in range(groups + 1):

                    def prepare(j):
                        def along_y(base):
                            def row(k):
                                at = slice(base + k, base + k + 8)
                                return along[p, at, j * LANES : (j + 1) * LANES]

                            return taps(row(0), row(d) + row(-d), row(d2) + row(-d2))

                        if g == groups:
                            t = jnp.where(top, along_y(2 * rows), along_y(rows - 8))
                        else:
                            t = along_y(rows + 8 * g)
                        return (t,) + tuple(
                            pltpu.roll(t, shift, 1) for shift in (LANES - d, LANES - d2, d, d2)
                        )

                    ready = {j: prepare(j) for j in (tiles - 1, 0)}
                    for j in range(tiles):
                        n, m = (j + 1) % tiles, (j - 1) % tiles
                        if n not in ready:
                            ready[n] = prepare(n)
                        t, l1, l2, r1, r2 = ready[j]
                        near = jnp.where(up1, l1, ready[n][1]) + jnp.where(dn1, r1, ready[m][3])
                        far = jnp.where(up2, l2, ready[n][2]) + jnp.where(dn2, r2, ready[m][4])
                        t = taps(t, near, far, 4.0)
                        for r in (0, rows + 8) if g == groups else (8 + 8 * g,):
                            smooth[p, r : r + 8, j * LANES : (j + 1) * LANES] = t
                return c

            lax.fori_loop(0, depth + 2, xy_body, 0)

        for spacing in range(1, DMAX + 1):
            pl.when(d == spacing)(functools.partial(xy_pass, spacing))

        first, last = lane == 0, lane == LANES - 1

        def hess_body(z, c):
            def prepare(j):
                def at(dz, g):
                    return smooth[z + 1 + dz, 8 * g : 8 * g + 8, j * LANES : (j + 1) * LANES]

                centre = [at(0, g) for g in range(groups + 2)]
                above = [at(1, g) for g in range(groups + 2)]
                below = [at(-1, g) for g in range(groups + 2)]
                slope = [a - b for a, b in zip(above, below)]

                def beside(v, g):
                    up = pltpu.roll(jnp.where(top, v[g + 1], v[g]), 7, 0)
                    down = pltpu.roll(jnp.where(bottom, v[g - 1], v[g]), 1, 0)
                    return up, down

                results = []
                for g in range(1, groups + 1):
                    up, down = beside(centre, g)
                    slope_up, slope_down = beside(slope, g)
                    twice = centre[g] + centre[g]
                    hzz = (above[g] + below[g]) - twice
                    hyy = (up + down) - twice
                    zy = slope_up - slope_down
                    shifted = [
                        (pltpu.roll(v, LANES - 1, 1), pltpu.roll(v, 1, 1))
                        for v in (centre[g], slope[g], up - down)
                    ]
                    results.append((twice, hzz, hyy, zy, shifted))
                return results

            def finish(j, r, low, mid, high):
                twice, hzz, hyy, zy, shifted = mid
                plus = [jnp.where(last, high[4][i][0], shifted[i][0]) for i in range(3)]
                minus = [jnp.where(first, low[4][i][1], shifted[i][1]) for i in range(3)]
                hxx = (plus[0] + minus[0]) - twice
                zx = plus[1] - minus[1]
                yx = plus[2] - minus[2]
                flat = hxx + hyy
                trace = flat + hzz
                squares = 0.0625 * (zy * zy + zx * zx + yx * yx)
                minors = hxx * hyy + flat * hzz - squares
                value = (trace * trace * (1.0 / 3.0) - minors) / (1.0 + jnp.exp(trace))
                lanes = slice((j - 1) * LANES, j * LANES)
                resp[z, r : r + 8, lanes] = jnp.maximum(resp[z, r : r + 8, lanes], value)
                feature[pl.ds(pl.multiple_of(z * rows + r, 8), 8), lanes] = value

            ready = [prepare(0), prepare(1)]
            for j in range(1, tiles - 1):
                ready.append(prepare(j + 1))
                for g in range(groups):
                    finish(j, 8 * g, *[ready[j + i][g] for i in (-1, 0, 1)])
            return c

        lax.fori_loop(0, depth, hess_body, 0)

        xcell = xcell_ref[...]
        slots = xcell.shape[0]
        chunk = 256

        def gather_body(i, acc):
            x0 = pl.multiple_of(i * chunk, chunk)
            block = feature[:, pl.ds(x0, chunk)]
            high = block.astype(jnp.bfloat16)
            rest = (block - high.astype(jnp.float32)).astype(jnp.bfloat16)
            block = jnp.concatenate([high, rest, high], axis=0)
            where = lax.broadcasted_iota(jnp.int32, (slots, chunk), 1) + x0
            where = where + (first_tile + 1) * LANES
            where = jnp.where(where >= width, where - width, where)
            for dx in range(2):
                cell = xcell + dx
                cell = jnp.where(cell == width, 0, cell)
                picked = jnp.dot(chosen[dx], block, preferred_element_type=jnp.float32)
                acc = acc + jnp.sum(jnp.where(where == cell, picked, 0.0), axis=1, keepdims=True)
            return acc

        partial = lax.fori_loop(0, kept // chunk, gather_body, jnp.zeros((slots, 1), jnp.float32))
        column = lax.broadcasted_iota(jnp.int32, (slots, cat_ref.shape[2]), 1)
        spread = jnp.where(column == column_ref[...], partial, 0.0)
        cat_ref[level] = jnp.sum(spread, axis=0, keepdims=True)
        return carry

    lax.fori_loop(0, SCALES, level_body, 0)

    until = min(kept, width - (first_tile + 1) * LANES)
    outs = [(0, (first_tile + 1) * LANES, until)]
    if until < kept:
        outs.append((until, 0, kept - until))
    copies = [
        pltpu.make_async_copy(
            resp.at[:, :, pl.ds(low, size)], out_ref.at[:, :, pl.ds(to, size)], sems.at[n]
        )
        for n, (low, to, size) in enumerate(outs)
    ]
    for copy in copies:
        copy.start()
    for copy in copies:
        copy.wait()


def ring(axis, step):
    count = lax.axis_size(axis)
    return [(i, (i + step) % count) for i in range(count)]


def per_device(density, dilations, owner_rank, owner_slot, base_cell, corner_weights):
    depth, rows, width = density.shape
    groups = lax.axis_size("gy")

    half = width // 2

    def z_sides(block):
        low = lax.ppermute(block[depth - HALO :], "gz", ring("gz", 1))
        high = lax.ppermute(block[:HALO], "gz", ring("gz", -1))
        return low, high

    def y_sides(block):
        sides = [lax.ppermute(block, "gy", ring("gy", 1))]
        if groups != 2:
            sides.append(lax.ppermute(block, "gy", ring("gy", -1)))
        return sides

    front = density[:, :, :half]
    beside = y_sides(front)
    low, high = z_sides(front)
    beside, back = lax.optimization_barrier((beside, density[:, :, half:]))
    parts_a = [low, density, high]
    beside_b = y_sides(back)
    for band in beside:
        low, high = z_sides(band)
        parts_a += [low, band, high]
    low, high = z_sides(back)
    parts_b = [low, density, high]
    beside_b, parts_a = lax.optimization_barrier((beside_b, parts_a))
    for band in beside_b:
        low, high = z_sides(band)
        parts_b += [low, band, high]
    bands = 1 + len(beside)

    plane = (rows - 1) * width
    z_index = base_cell // plane
    remainder = base_cell % plane
    y_index = remainder // width
    x_index = remainder % width
    row_at = jnp.arange(depth * rows, dtype=jnp.int32)[None, :]
    select = []
    for step_x in (0, 1):
        chosen = 0.0
        for step_z in (0, 1):
            for step_y in (0, 1):
                row = (z_index + step_z) * rows + y_index + step_y
                weight = corner_weights[4 * step_z + 2 * step_y + step_x]
                chosen = chosen + jnp.where(row[:, None] == row_at, weight[:, None], 0.0)
        select.append(chosen)
    select = jnp.stack(select)
    column = owner_rank * HOWN + owner_slot[:, None]

    vmem = pl.BlockSpec(memory_space=pltpu.VMEM)
    anywhere = pl.BlockSpec(memory_space=pl.ANY)
    half_tiles = half // LANES

    def run(tiles, first_tile, pieces, parts, onto):
        cells = depth * rows * tiles * LANES
        operands = [dilations, select, x_index[:, None], column] + parts
        in_specs = [pl.BlockSpec(memory_space=pltpu.SMEM), vmem, vmem, vmem]
        in_specs += [anywhere] * len(parts)
        aliases = {}
        if onto is not None:
            aliases = {len(operands): 0}
            operands.append(onto)
            in_specs.append(anywhere)
        return pl.pallas_call(
            functools.partial(
                kernel, depth, rows, bands, tiles, first_tile, width, pieces, onto is not None
            ),
            out_shape=(
                jax.ShapeDtypeStruct((depth, rows, width), jnp.float32),
                jax.ShapeDtypeStruct((SCALES, 1, groups * HOWN), jnp.float32),
            ),
            in_specs=in_specs,
            out_specs=(anywhere, vmem),
            input_output_aliases=aliases,
            scratch_shapes=[
                pltpu.VMEM((depth + 2 * HALO, bands * rows, tiles * LANES), jnp.float32),
                pltpu.VMEM((depth + 2, 3 * rows, tiles * LANES), jnp.float32),
                pltpu.VMEM((depth + 2, rows + 16, tiles * LANES), jnp.float32),
                pltpu.VMEM((depth * rows, (tiles - 2) * LANES), jnp.float32),
                pltpu.VMEM((2, base_cell.shape[0], 3 * depth * rows), jnp.bfloat16),
                pltpu.VMEM((depth, rows, (tiles - 2) * LANES), jnp.float32),
                pltpu.SemaphoreType.DMA((len(parts),)),
            ],
            compiler_params=pltpu.CompilerParams(vmem_limit_bytes=48 * 1024 * 1024),
            cost_estimate=pl.CostEstimate(
                flops=cells * SCALES * 100,
                bytes_accessed=cells * 4 * 8,
                transcendentals=cells * SCALES,
            ),
        )(*operands)

    edge = 2 * LANES
    pieces_a = (((0, 0), half, 0),)
    pieces_b = (
        ((half - edge, half - edge), edge, 0),
        ((0, half), half, edge),
        ((0, 0), edge, edge + half),
    )
    response, spread_a = run(half_tiles, 0, pieces_a, parts_a, None)
    response, spread_b = run(
        half_tiles + 4, half_tiles - 2, pieces_b, parts_a + parts_b + parts_a, response
    )
    spread = spread_a + spread_b

    spread = spread[:, 0]
    me = lax.axis_index("gy")

    def share(owner):
        return lax.dynamic_slice_in_dim(spread, owner * HOWN, HOWN, axis=1)

    catalogue = share(me)
    for step in range(1, groups):
        catalogue = catalogue + lax.ppermute(
            share((me + step) % groups), "gy", ring("gy", step)
        )
    return (response, catalogue)


def solution(mesh):
    placed = (
        P("gz", "gy", None),
        P(),
        P(("gz", "gy"), None),
        P(("gz", "gy")),
        P(("gz", "gy")),
        P(None, ("gz", "gy")),
    )
    return jax.shard_map(
        per_device,
        mesh=mesh,
        in_specs=placed,
        out_specs=(P("gz", "gy", None), P(None, ("gz", "gy"))),
        check_vma=False,
    )
```

```python
import functools

import jax
import jax.numpy as jnp
from jax import lax
from jax.experimental import pallas as pl
from jax.experimental.pallas import tpu as pltpu
from jax.sharding import PartitionSpec as P

SCALES = 3
HALO = 9
HOWN = 256
DMAX = 4
LANES = 128
TAPS = (0.375, 0.25, 0.0625)


def taps(centre, near, far, scale=1.0):
    return (TAPS[0] * scale) * centre + (TAPS[1] * scale) * near + (TAPS[2] * scale) * far


def kernel(depth, rows, bands, tiles, first_tile, width, pieces, aliased, *refs):
    dil_ref, select_ref, xcell_ref, column_ref = refs[:4]
    count = 4 + 3 * bands * len(pieces)
    parts = refs[4:count]
    if aliased:
        count += 1
    out_ref, cat_ref, field, along, smooth, feature, chosen, resp, sems = refs[count:]
    span = tiles * LANES
    kept = span - 2 * LANES
    starts = (0, HALO, HALO + depth)
    copies = []
    for n, (low, size, to) in enumerate(pieces):
        for b in range(bands):
            for i in range(3):
                src = parts[(n * bands + b) * 3 + i]
                planes = depth if i == 1 else HALO
                copies.append(
                    pltpu.make_async_copy(
                        src.at[:, :, pl.ds(low[src.shape[2] == width], size)],
                        field.at[pl.ds(starts[i], planes), pl.ds(b * rows, rows), pl.ds(to, size)],
                        sems.at[len(copies)],
                    )
                )
    for copy in copies:
        copy.start()
    resp[...] = jnp.full(resp.shape, -jnp.inf, jnp.float32)
    for dx in range(2):
        weights = select_ref[dx]
        high = weights.astype(jnp.bfloat16)
        rest = (weights - high.astype(jnp.float32)).astype(jnp.bfloat16)
        slots = weights.shape[0]
        chosen[dx * slots : (dx + 1) * slots] = jnp.concatenate([high, high, rest], axis=1)
    for copy in copies:
        copy.wait()

    places = ((rows,), (0, 2 * rows)) if bands == 2 else ((rows,), (0,), (2 * rows,))
    lane = lax.broadcasted_iota(jnp.int32, (8, LANES), 1)
    groups = rows // 8
    sub = lax.broadcasted_iota(jnp.int32, (8, LANES), 0)
    top, bottom = sub == 0, sub == 7

    def level_body(level, carry):
        d = dil_ref[level]
        d2 = 2 * d

        def z_body(p, c):
            at = p + HALO - 1
            for b in range(bands):
                for r in range(0, rows, 8):
                    for x in range(0, span, 512):
                        def plane(k):
                            return field[at + k, b * rows + r : b * rows + r + 8, x : x + 512]

                        v = taps(plane(0), plane(d) + plane(-d), plane(d2) + plane(-d2))
                        for place in places[b]:
                            along[p, place + r : place + r + 8, x : x + 512] = v
            return c

        lax.fori_loop(0, depth + 2, z_body, 0)

        def xy_pass(d):
            d2 = 2 * d
            up1, up2 = lane < LANES - d, lane < LANES - d2
            dn1, dn2 = lane >= d, lane >= d2

            def xy_body(p, c):
                for g in range(groups + 1):

                    def prepare(j):
                        def along_y(base):
                            def row(k):
                                at = slice(base + k, base + k + 8)
                                return along[p, at, j * LANES : (j + 1) * LANES]

                            return taps(row(0), row(d) + row(-d), row(d2) + row(-d2))

                        if g == groups:
                            t = jnp.where(top, along_y(2 * rows), along_y(rows - 8))
                        else:
                            t = along_y(rows + 8 * g)
                        return (t,) + tuple(
                            pltpu.roll(t, shift, 1) for shift in (LANES - d, LANES - d2, d, d2)
                        )

                    ready = {j: prepare(j) for j in (tiles - 1, 0)}
                    for j in range(tiles):
                        n, m = (j + 1) % tiles, (j - 1) % tiles
                        if n not in ready:
                            ready[n] = prepare(n)
                        t, l1, l2, r1, r2 = ready[j]
                        near = jnp.where(up1, l1, ready[n][1]) + jnp.where(dn1, r1, ready[m][3])
                        far = jnp.where(up2, l2, ready[n][2]) + jnp.where(dn2, r2, ready[m][4])
                        t = taps(t, near, far, 4.0)
                        for r in (0, rows + 8) if g == groups else (8 + 8 * g,):
                            smooth[p, r : r + 8, j * LANES : (j + 1) * LANES] = t
                return c

            lax.fori_loop(0, depth + 2, xy_body, 0)

        for spacing in range(1, DMAX + 1):
            pl.when(d == spacing)(functools.partial(xy_pass, spacing))

        first, last = lane == 0, lane == LANES - 1

        def hess_body(z, c):
            def prepare(j):
                def at(dz, g):
                    return smooth[z + 1 + dz, 8 * g : 8 * g + 8, j * LANES : (j + 1) * LANES]

                centre = [at(0, g) for g in range(groups + 2)]
                above = [at(1, g) for g in range(groups + 2)]
                below = [at(-1, g) for g in range(groups + 2)]
                slope = [a - b for a, b in zip(above, below)]

                def beside(v, g):
                    up = pltpu.roll(jnp.where(top, v[g + 1], v[g]), 7, 0)
                    down = pltpu.roll(jnp.where(bottom, v[g - 1], v[g]), 1, 0)
                    return up, down

                results = []
                for g in range(1, groups + 1):
                    up, down = beside(centre, g)
                    slope_up, slope_down = beside(slope, g)
                    twice = centre[g] + centre[g]
                    hzz = (above[g] + below[g]) - twice
                    hyy = (up + down) - twice
                    zy = slope_up - slope_down
                    shifted = [
                        (pltpu.roll(v, LANES - 1, 1), pltpu.roll(v, 1, 1))
                        for v in (centre[g], slope[g], up - down)
                    ]
                    results.append((twice, hzz, hyy, zy, shifted))
                return results

            def finish(j, r, low, mid, high):
                twice, hzz, hyy, zy, shifted = mid
                plus = [jnp.where(last, high[4][i][0], shifted[i][0]) for i in range(3)]
                minus = [jnp.where(first, low[4][i][1], shifted[i][1]) for i in range(3)]
                hxx = (plus[0] + minus[0]) - twice
                zx = plus[1] - minus[1]
                yx = plus[2] - minus[2]
                flat = hxx + hyy
                trace = flat + hzz
                squares = 0.0625 * (zy * zy + zx * zx + yx * yx)
                minors = hxx * hyy + flat * hzz - squares
                value = (trace * trace * (1.0 / 3.0) - minors) / (1.0 + jnp.exp(trace))
                lanes = slice((j - 1) * LANES, j * LANES)
                resp[z, r : r + 8, lanes] = jnp.maximum(resp[z, r : r + 8, lanes], value)
                feature[pl.ds(pl.multiple_of(z * rows + r, 8), 8), lanes] = value

            ready = [prepare(0), prepare(1)]
            for j in range(1, tiles - 1):
                ready.append(prepare(j + 1))
                for g in range(groups):
                    finish(j, 8 * g, *[ready[j + i][g] for i in (-1, 0, 1)])
            return c

        lax.fori_loop(0, depth, hess_body, 0)

        xcell = xcell_ref[...]
        slots = xcell.shape[0]
        chunk = 256

        def gather_body(i, acc):
            x0 = pl.multiple_of(i * chunk, chunk)
            block = feature[:, pl.ds(x0, chunk)]
            high = block.astype(jnp.bfloat16)
            rest = (block - high.astype(jnp.float32)).astype(jnp.bfloat16)
            block = jnp.concatenate([high, rest, high], axis=0)
            where = lax.broadcasted_iota(jnp.int32, (slots, chunk), 1) + x0
            where = where + (first_tile + 1) * LANES
            where = jnp.where(where >= width, where - width, where)
            picked = jnp.dot(chosen[...], block, preferred_element_type=jnp.float32)
            kept_cells = 0.0
            for dx in range(2):
                cell = xcell + dx
                cell = jnp.where(cell == width, 0, cell)
                corner = picked[dx * slots : (dx + 1) * slots]
                kept_cells = kept_cells + jnp.where(where == cell, corner, 0.0)
            acc = acc + jnp.sum(kept_cells, axis=1, keepdims=True)
            return acc

        partial = lax.fori_loop(0, kept // chunk, gather_body, jnp.zeros((slots, 1), jnp.float32))
        column = lax.broadcasted_iota(jnp.int32, (slots, cat_ref.shape[2]), 1)
        spread = jnp.where(column == column_ref[...], partial, 0.0)
        cat_ref[level] = jnp.sum(spread, axis=0, keepdims=True)
        return carry

    lax.fori_loop(0, SCALES, level_body, 0)

    until = min(kept, width - (first_tile + 1) * LANES)
    outs = [(0, (first_tile + 1) * LANES, until)]
    if until < kept:
        outs.append((until, 0, kept - until))
    copies = [
        pltpu.make_async_copy(
            resp.at[:, :, pl.ds(low, size)], out_ref.at[:, :, pl.ds(to, size)], sems.at[n]
        )
        for n, (low, to, size) in enumerate(outs)
    ]
    for copy in copies:
        copy.start()
    for copy in copies:
        copy.wait()


def ring(axis, step):
    count = lax.axis_size(axis)
    return [(i, (i + step) % count) for i in range(count)]


def per_device(density, dilations, owner_rank, owner_slot, base_cell, corner_weights):
    depth, rows, width = density.shape
    groups = lax.axis_size("gy")

    half = width // 2

    def z_sides(block):
        low = lax.ppermute(block[depth - HALO :], "gz", ring("gz", 1))
        high = lax.ppermute(block[:HALO], "gz", ring("gz", -1))
        return low, high

    def y_sides(block):
        sides = [lax.ppermute(block, "gy", ring("gy", 1))]
        if groups != 2:
            sides.append(lax.ppermute(block, "gy", ring("gy", -1)))
        return sides

    front = density[:, :, :half]
    beside = y_sides(front)
    low, high = z_sides(front)
    beside, back = lax.optimization_barrier((beside, density[:, :, half:]))
    parts_a = [low, density, high]
    for band in beside:
        low, high = z_sides(band)
        parts_a += [low, band, high]

    def across(block, step_z, step_y):
        slabs = lax.axis_size("gz")
        pairs = [
            (z * groups + y, (z + step_z) % slabs * groups + (y + step_y) % groups)
            for z in range(slabs)
            for y in range(groups)
        ]
        return lax.ppermute(block, ("gz", "gy"), pairs)

    last_planes, first_planes = back[depth - HALO :], back[:HALO]
    low, high = z_sides(back)
    parts_b = [low, density, high]
    for band, step in zip(y_sides(back), (1, -1)):
        low, high = across(last_planes, 1, step), across(first_planes, -1, step)
        parts_b += [low, band, high]
    bands = 1 + len(beside)

    plane = (rows - 1) * width
    z_index = base_cell // plane
    remainder = base_cell % plane
    y_index = remainder // width
    x_index = remainder % width
    row_at = jnp.arange(depth * rows, dtype=jnp.int32)[None, :]
    select = []
    for step_x in (0, 1):
        chosen = 0.0
        for step_z in (0, 1):
            for step_y in (0, 1):
                row = (z_index + step_z) * rows + y_index + step_y
                weight = corner_weights[4 * step_z + 2 * step_y + step_x]
                chosen = chosen + jnp.where(row[:, None] == row_at, weight[:, None], 0.0)
        select.append(chosen)
    select = jnp.stack(select)
    column = owner_rank * HOWN + owner_slot[:, None]

    vmem = pl.BlockSpec(memory_space=pltpu.VMEM)
    anywhere = pl.BlockSpec(memory_space=pl.ANY)
    half_tiles = half // LANES

    def run(tiles, first_tile, pieces, parts, onto):
        cells = depth * rows * tiles * LANES
        operands = [dilations, select, x_index[:, None], column] + parts
        in_specs = [pl.BlockSpec(memory_space=pltpu.SMEM), vmem, vmem, vmem]
        in_specs += [anywhere] * len(parts)
        aliases = {}
        if onto is not None:
            aliases = {len(operands): 0}
            operands.append(onto)
            in_specs.append(anywhere)
        return pl.pallas_call(
            functools.partial(
                kernel, depth, rows, bands, tiles, first_tile, width, pieces, onto is not None
            ),
            out_shape=(
                jax.ShapeDtypeStruct((depth, rows, width), jnp.float32),
                jax.ShapeDtypeStruct((SCALES, 1, groups * HOWN), jnp.float32),
            ),
            in_specs=in_specs,
            out_specs=(anywhere, vmem),
            input_output_aliases=aliases,
            scratch_shapes=[
                pltpu.VMEM((depth + 2 * HALO, bands * rows, tiles * LANES), jnp.float32),
                pltpu.VMEM((depth + 2, 3 * rows, tiles * LANES), jnp.float32),
                pltpu.VMEM((depth + 2, rows + 16, tiles * LANES), jnp.float32),
                pltpu.VMEM((depth * rows, (tiles - 2) * LANES), jnp.float32),
                pltpu.VMEM((2 * base_cell.shape[0], 3 * depth * rows), jnp.bfloat16),
                pltpu.VMEM((depth, rows, (tiles - 2) * LANES), jnp.float32),
                pltpu.SemaphoreType.DMA((len(parts),)),
            ],
            compiler_params=pltpu.CompilerParams(vmem_limit_bytes=48 * 1024 * 1024),
            cost_estimate=pl.CostEstimate(
                flops=cells * SCALES * 100,
                bytes_accessed=cells * 4 * 8,
                transcendentals=cells * SCALES,
            ),
        )(*operands)

    edge = 2 * LANES
    pieces_a = (((0, 0), half, 0),)
    pieces_b = (
        ((half - edge, half - edge), edge, 0),
        ((0, half), half, edge),
        ((0, 0), edge, edge + half),
    )
    response, spread_a = run(half_tiles, 0, pieces_a, parts_a, None)
    response, spread_b = run(
        half_tiles + 4, half_tiles - 2, pieces_b, parts_a + parts_b + parts_a, response
    )
    spread = spread_a + spread_b

    spread = spread[:, 0]
    me = lax.axis_index("gy")

    def share(owner):
        return lax.dynamic_slice_in_dim(spread, owner * HOWN, HOWN, axis=1)

    catalogue = share(me)
    for step in range(1, groups):
        catalogue = catalogue + lax.ppermute(
            share((me + step) % groups), "gy", ring("gy", step)
        )
    return (response, catalogue)


def solution(mesh):
    placed = (
        P("gz", "gy", None),
        P(),
        P(("gz", "gy"), None),
        P(("gz", "gy")),
        P(("gz", "gy")),
        P(None, ("gz", "gy")),
    )
    return jax.shard_map(
        per_device,
        mesh=mesh,
        in_specs=placed,
        out_specs=(P("gz", "gy", None), P(None, ("gz", "gy"))),
        check_vma=False,
    )
```

```python
import functools

import jax
import jax.numpy as jnp
from jax import lax
from jax.experimental import pallas as pl
from jax.experimental.pallas import tpu as pltpu
from jax.sharding import PartitionSpec as P

SCALES = 3
HALO = 9
HOWN = 256
DMAX = 4
LANES = 128
TAPS = (0.375, 0.25, 0.0625)


def taps(centre, near, far, scale=1.0):
    return (TAPS[0] * scale) * centre + (TAPS[1] * scale) * near + (TAPS[2] * scale) * far


def kernel(depth, rows, bands, tiles, first_tile, width, pieces, aliased, *refs):
    dil_ref, select_ref, xcell_ref, column_ref = refs[:4]
    count = 4 + 3 * bands * len(pieces)
    parts = refs[4:count]
    if aliased:
        count += 1
    out_ref, cat_ref, field, along, smooth, feature, chosen, resp, sems = refs[count:]
    span = tiles * LANES
    kept = span - 2 * LANES
    starts = (0, HALO, HALO + depth)
    copies = []
    for n, (low, size, to) in enumerate(pieces):
        for b in range(bands):
            for i in range(3):
                src = parts[(n * bands + b) * 3 + i]
                planes = depth if i == 1 else HALO
                copies.append(
                    pltpu.make_async_copy(
                        src.at[:, :, pl.ds(low[src.shape[2] == width], size)],
                        field.at[pl.ds(starts[i], planes), pl.ds(b * rows, rows), pl.ds(to, size)],
                        sems.at[len(copies)],
                    )
                )
    for copy in copies:
        copy.start()
    resp[...] = jnp.full(resp.shape, -jnp.inf, jnp.float32)
    for dx in range(2):
        weights = select_ref[dx]
        high = weights.astype(jnp.bfloat16)
        rest = (weights - high.astype(jnp.float32)).astype(jnp.bfloat16)
        slots = weights.shape[0]
        chosen[dx * slots : (dx + 1) * slots] = jnp.concatenate([high, high, rest], axis=1)
    for copy in copies:
        copy.wait()

    places = ((rows,), (0, 2 * rows)) if bands == 2 else ((rows,), (0,), (2 * rows,))
    lane = lax.broadcasted_iota(jnp.int32, (8, LANES), 1)
    groups = rows // 8
    sub = lax.broadcasted_iota(jnp.int32, (8, LANES), 0)
    top, bottom = sub == 0, sub == 7

    def level_body(level, carry):
        d = dil_ref[level]
        d2 = 2 * d

        def z_body(p, c):
            at = p + HALO - 1
            for b in range(bands):
                for r in range(0, rows, 8):
                    for x in range(0, span, 256):
                        def plane(k):
                            return field[at + k, b * rows + r : b * rows + r + 8, x : x + 256]

                        v = taps(plane(0), plane(d) + plane(-d), plane(d2) + plane(-d2))
                        for place in places[b]:
                            along[p, place + r : place + r + 8, x : x + 256] = v
            return c

        lax.fori_loop(0, depth + 2, z_body, 0)

        def xy_pass(d):
            d2 = 2 * d
            up1, up2 = lane < LANES - d, lane < LANES - d2
            dn1, dn2 = lane >= d, lane >= d2

            def xy_body(p, c):
                for g in range(groups + 1):

                    def prepare(j):
                        def along_y(base):
                            def row(k):
                                at = slice(base + k, base + k + 8)
                                return along[p, at, j * LANES : (j + 1) * LANES]

                            return taps(row(0), row(d) + row(-d), row(d2) + row(-d2))

                        if g == groups:
                            t = jnp.where(top, along_y(2 * rows), along_y(rows - 8))
                        else:
                            t = along_y(rows + 8 * g)
                        return (t,) + tuple(
                            pltpu.roll(t, shift, 1) for shift in (LANES - d, LANES - d2, d, d2)
                        )

                    ready = {j: prepare(j) for j in (tiles - 1, 0)}
                    for j in range(tiles):
                        n, m = (j + 1) % tiles, (j - 1) % tiles
                        if n not in ready:
                            ready[n] = prepare(n)
                        t, l1, l2, r1, r2 = ready[j]
                        near = jnp.where(up1, l1, ready[n][1]) + jnp.where(dn1, r1, ready[m][3])
                        far = jnp.where(up2, l2, ready[n][2]) + jnp.where(dn2, r2, ready[m][4])
                        t = taps(t, near, far, 4.0)
                        for r in (0, rows + 8) if g == groups else (8 + 8 * g,):
                            smooth[p, r : r + 8, j * LANES : (j + 1) * LANES] = t
                return c

            lax.fori_loop(0, depth + 2, xy_body, 0)

        for spacing in range(1, DMAX + 1):
            pl.when(d == spacing)(functools.partial(xy_pass, spacing))

        first, last = lane == 0, lane == LANES - 1

        def hess_body(z, c):
            def prepare(j):
                def at(dz, g):
                    return smooth[z + 1 + dz, 8 * g : 8 * g + 8, j * LANES : (j + 1) * LANES]

                centre = [at(0, g) for g in range(groups + 2)]
                above = [at(1, g) for g in range(groups + 2)]
                below = [at(-1, g) for g in range(groups + 2)]
                slope = [a - b for a, b in zip(above, below)]

                def beside(v, g):
                    up = pltpu.roll(jnp.where(top, v[g + 1], v[g]), 7, 0)
                    down = pltpu.roll(jnp.where(bottom, v[g - 1], v[g]), 1, 0)
                    return up, down

                results = []
                for g in range(1, groups + 1):
                    up, down = beside(centre, g)
                    slope_up, slope_down = beside(slope, g)
                    twice = centre[g] + centre[g]
                    hzz = (above[g] + below[g]) - twice
                    hyy = (up + down) - twice
                    zy = slope_up - slope_down
                    shifted = [
                        (pltpu.roll(v, LANES - 1, 1), pltpu.roll(v, 1, 1))
                        for v in (centre[g], slope[g], up - down)
                    ]
                    results.append((twice, hzz, hyy, zy, shifted))
                return results

            def finish(j, r, low, mid, high):
                twice, hzz, hyy, zy, shifted = mid
                plus = [jnp.where(last, high[4][i][0], shifted[i][0]) for i in range(3)]
                minus = [jnp.where(first, low[4][i][1], shifted[i][1]) for i in range(3)]
                hxx = (plus[0] + minus[0]) - twice
                zx = plus[1] - minus[1]
                yx = plus[2] - minus[2]
                flat = hxx + hyy
                trace = flat + hzz
                squares = 0.0625 * (zy * zy + zx * zx + yx * yx)
                minors = hxx * hyy + flat * hzz - squares
                value = (trace * trace * (1.0 / 3.0) - minors) * (0.5 - 0.5 * jnp.tanh(0.5 * trace))
                lanes = slice((j - 1) * LANES, j * LANES)
                resp[z, r : r + 8, lanes] = jnp.maximum(resp[z, r : r + 8, lanes], value)
                feature[pl.ds(pl.multiple_of(z * rows + r, 8), 8), lanes] = value

            ready = [prepare(0), prepare(1)]
            for j in range(1, tiles - 1):
                ready.append(prepare(j + 1))
                for g in range(groups):
                    finish(j, 8 * g, *[ready[j + i][g] for i in (-1, 0, 1)])
            return c

        lax.fori_loop(0, depth, hess_body, 0)

        xcell = xcell_ref[...]
        slots = xcell.shape[0]
        chunk = 256

        def gather_body(i, acc):
            x0 = pl.multiple_of(i * chunk, chunk)
            block = feature[:, pl.ds(x0, chunk)]
            high = block.astype(jnp.bfloat16)
            rest = (block - high.astype(jnp.float32)).astype(jnp.bfloat16)
            block = jnp.concatenate([high, rest, high], axis=0)
            where = lax.broadcasted_iota(jnp.int32, (slots, chunk), 1) + x0
            where = where + (first_tile + 1) * LANES
            where = jnp.where(where >= width, where - width, where)
            picked = jnp.dot(chosen[...], block, preferred_element_type=jnp.float32)
            kept_cells = 0.0
            for dx in range(2):
                cell = xcell + dx
                cell = jnp.where(cell == width, 0, cell)
                corner = picked[dx * slots : (dx + 1) * slots]
                kept_cells = kept_cells + jnp.where(where == cell, corner, 0.0)
            acc = acc + jnp.sum(kept_cells, axis=1, keepdims=True)
            return acc

        partial = lax.fori_loop(0, kept // chunk, gather_body, jnp.zeros((slots, 1), jnp.float32))
        column = lax.broadcasted_iota(jnp.int32, (slots, cat_ref.shape[2]), 1)
        spread = jnp.where(column == column_ref[...], partial, 0.0)
        cat_ref[level] = jnp.sum(spread, axis=0, keepdims=True)
        return carry

    lax.fori_loop(0, SCALES, level_body, 0)

    until = min(kept, width - (first_tile + 1) * LANES)
    outs = [(0, (first_tile + 1) * LANES, until)]
    if until < kept:
        outs.append((until, 0, kept - until))
    copies = [
        pltpu.make_async_copy(
            resp.at[:, :, pl.ds(low, size)], out_ref.at[:, :, pl.ds(to, size)], sems.at[n]
        )
        for n, (low, to, size) in enumerate(outs)
    ]
    for copy in copies:
        copy.start()
    for copy in copies:
        copy.wait()


def ring(axis, step):
    count = lax.axis_size(axis)
    return [(i, (i + step) % count) for i in range(count)]


def per_device(density, dilations, owner_rank, owner_slot, base_cell, corner_weights):
    depth, rows, width = density.shape
    groups = lax.axis_size("gy")

    half = width * 5 // 8 // LANES * LANES

    def z_sides(block):
        low = lax.ppermute(block[depth - HALO :], "gz", ring("gz", 1))
        high = lax.ppermute(block[:HALO], "gz", ring("gz", -1))
        return low, high

    def y_sides(block):
        sides = [lax.ppermute(block, "gy", ring("gy", 1))]
        if groups != 2:
            sides.append(lax.ppermute(block, "gy", ring("gy", -1)))
        return sides

    front = density[:, :, :half]
    beside = y_sides(front)
    low, high = z_sides(front)
    beside, back = lax.optimization_barrier((beside, density[:, :, half:]))
    parts_a = [low, density, high]
    beside_b = y_sides(back)
    for band in beside:
        low, high = z_sides(band)
        parts_a += [low, band, high]
    low, high = z_sides(back)
    parts_b = [low, density, high]
    beside_b, parts_a = lax.optimization_barrier((beside_b, parts_a))
    for band in beside_b:
        low, high = z_sides(band)
        parts_b += [low, band, high]
    bands = 1 + len(beside)

    plane = (rows - 1) * width
    z_index = base_cell // plane
    remainder = base_cell % plane
    y_index = remainder // width
    x_index = remainder % width
    row_at = jnp.arange(depth * rows, dtype=jnp.int32)[None, :]
    select = []
    for step_x in (0, 1):
        chosen = 0.0
        for step_z in (0, 1):
            for step_y in (0, 1):
                row = (z_index + step_z) * rows + y_index + step_y
                weight = corner_weights[4 * step_z + 2 * step_y + step_x]
                chosen = chosen + jnp.where(row[:, None] == row_at, weight[:, None], 0.0)
        select.append(chosen)
    select = jnp.stack(select)
    column = owner_rank * HOWN + owner_slot[:, None]

    vmem = pl.BlockSpec(memory_space=pltpu.VMEM)
    anywhere = pl.BlockSpec(memory_space=pl.ANY)
    half_tiles = half // LANES
    rest_tiles = width // LANES - half_tiles

    def run(tiles, first_tile, pieces, parts, onto):
        cells = depth * rows * tiles * LANES
        operands = [dilations, select, x_index[:, None], column] + parts
        in_specs = [pl.BlockSpec(memory_space=pltpu.SMEM), vmem, vmem, vmem]
        in_specs += [anywhere] * len(parts)
        aliases = {}
        if onto is not None:
            aliases = {len(operands): 0}
            operands.append(onto)
            in_specs.append(anywhere)
        return pl.pallas_call(
            functools.partial(
                kernel, depth, rows, bands, tiles, first_tile, width, pieces, onto is not None
            ),
            out_shape=(
                jax.ShapeDtypeStruct((depth, rows, width), jnp.float32),
                jax.ShapeDtypeStruct((SCALES, 1, groups * HOWN), jnp.float32),
            ),
            in_specs=in_specs,
            out_specs=(anywhere, vmem),
            input_output_aliases=aliases,
            scratch_shapes=[
                pltpu.VMEM((depth + 2 * HALO, bands * rows, tiles * LANES), jnp.float32),
                pltpu.VMEM((depth + 2, 3 * rows, tiles * LANES), jnp.float32),
                pltpu.VMEM((depth + 2, rows + 16, tiles * LANES), jnp.float32),
                pltpu.VMEM((depth * rows, (tiles - 2) * LANES), jnp.float32),
                pltpu.VMEM((2 * base_cell.shape[0], 3 * depth * rows), jnp.bfloat16),
                pltpu.VMEM((depth, rows, (tiles - 2) * LANES), jnp.float32),
                pltpu.SemaphoreType.DMA((len(parts),)),
            ],
            compiler_params=pltpu.CompilerParams(vmem_limit_bytes=48 * 1024 * 1024),
            cost_estimate=pl.CostEstimate(
                flops=cells * SCALES * 100,
                bytes_accessed=cells * 4 * 8,
                transcendentals=cells * SCALES,
            ),
        )(*operands)

    edge = 2 * LANES
    pieces_a = (((0, 0), half, 0),)
    pieces_b = (
        ((half - edge, half - edge), edge, 0),
        ((0, half), width - half, edge),
        ((0, 0), edge, edge + width - half),
    )
    response, spread_a = run(half_tiles, 0, pieces_a, parts_a, None)
    response, spread_b = run(
        rest_tiles + 4, half_tiles - 2, pieces_b, parts_a + parts_b + parts_a, response
    )
    spread = spread_a + spread_b

    spread = spread[:, 0]
    me = lax.axis_index("gy")

    def share(owner):
        return lax.dynamic_slice_in_dim(spread, owner * HOWN, HOWN, axis=1)

    catalogue = share(me)
    for step in range(1, groups):
        catalogue = catalogue + lax.ppermute(
            share((me + step) % groups), "gy", ring("gy", step)
        )
    return (response, catalogue)


def solution(mesh):
    placed = (
        P("gz", "gy", None),
        P(),
        P(("gz", "gy"), None),
        P(("gz", "gy")),
        P(("gz", "gy")),
        P(None, ("gz", "gy")),
    )
    return jax.shard_map(
        per_device,
        mesh=mesh,
        in_specs=placed,
        out_specs=(P("gz", "gy", None), P(None, ("gz", "gy"))),
        check_vma=False,
    )
```

```python
import functools

import jax
import jax.numpy as jnp
from jax import lax
from jax.experimental import pallas as pl
from jax.experimental.pallas import tpu as pltpu
from jax.sharding import PartitionSpec as P

SCALES = 3
HALO = 9
HOWN = 256
DMAX = 4
LANES = 128
TAPS = (0.375, 0.25, 0.0625)


def taps(centre, near, far, scale=1.0):
    return (TAPS[0] * scale) * centre + (TAPS[1] * scale) * near + (TAPS[2] * scale) * far


def kernel(depth, rows, bands, tiles, first_tile, width, pieces, aliased, *refs):
    dil_ref, select_ref, xcell_ref, column_ref = refs[:4]
    count = 4 + 3 * bands * len(pieces)
    parts = refs[4:count]
    if aliased:
        count += 1
    out_ref, cat_ref, field, along, smooth, feature, chosen, resp, sems = refs[count:]
    span = tiles * LANES
    kept = span - 2 * LANES
    starts = (0, HALO, HALO + depth)
    copies = []
    for n, (low, size, to) in enumerate(pieces):
        for b in range(bands):
            for i in range(3):
                src = parts[(n * bands + b) * 3 + i]
                planes = depth if i == 1 else HALO
                row = b * rows if src.shape[1] != rows else 0
                copies.append(
                    pltpu.make_async_copy(
                        src.at[:, pl.ds(row, rows), pl.ds(low[src.shape[2] == width], size)],
                        field.at[pl.ds(starts[i], planes), pl.ds(b * rows, rows), pl.ds(to, size)],
                        sems.at[len(copies)],
                    )
                )
    for copy in copies:
        copy.start()
    resp[...] = jnp.full(resp.shape, -jnp.inf, jnp.float32)
    for dx in range(2):
        weights = select_ref[dx]
        high = weights.astype(jnp.bfloat16)
        rest = (weights - high.astype(jnp.float32)).astype(jnp.bfloat16)
        slots = weights.shape[0]
        chosen[dx * slots : (dx + 1) * slots] = jnp.concatenate([high, high, rest], axis=1)
    for copy in copies:
        copy.wait()

    places = ((rows,), (0, 2 * rows)) if bands == 2 else ((rows,), (0,), (2 * rows,))
    lane = lax.broadcasted_iota(jnp.int32, (8, LANES), 1)
    groups = rows // 8
    sub = lax.broadcasted_iota(jnp.int32, (8, LANES), 0)
    top, bottom = sub == 0, sub == 7

    def level_body(level, carry):
        d = dil_ref[level]
        d2 = 2 * d

        def z_body(p, c):
            at = p + HALO - 1
            for b in range(bands):
                for r in range(0, rows, 8):
                    for x in range(0, span, 256):
                        def plane(k):
                            return field[at + k, b * rows + r : b * rows + r + 8, x : x + 256]

                        v = taps(plane(0), plane(d) + plane(-d), plane(d2) + plane(-d2))
                        for place in places[b]:
                            along[p, place + r : place + r + 8, x : x + 256] = v
            return c

        lax.fori_loop(0, depth + 2, z_body, 0)

        def xy_pass(d):
            d2 = 2 * d
            up1, up2 = lane < LANES - d, lane < LANES - d2
            dn1, dn2 = lane >= d, lane >= d2

            def xy_body(p, c):
                for g in range(groups + 1):

                    def prepare(j):
                        def along_y(base):
                            def row(k):
                                at = slice(base + k, base + k + 8)
                                return along[p, at, j * LANES : (j + 1) * LANES]

                            return taps(row(0), row(d) + row(-d), row(d2) + row(-d2))

                        if g == groups:
                            t = jnp.where(top, along_y(2 * rows), along_y(rows - 8))
                        else:
                            t = along_y(rows + 8 * g)
                        return (t,) + tuple(
                            pltpu.roll(t, shift, 1) for shift in (LANES - d, LANES - d2, d, d2)
                        )

                    ready = {j: prepare(j) for j in (tiles - 1, 0)}
                    for j in range(tiles):
                        n, m = (j + 1) % tiles, (j - 1) % tiles
                        if n not in ready:
                            ready[n] = prepare(n)
                        t, l1, l2, r1, r2 = ready[j]
                        near = jnp.where(up1, l1, ready[n][1]) + jnp.where(dn1, r1, ready[m][3])
                        far = jnp.where(up2, l2, ready[n][2]) + jnp.where(dn2, r2, ready[m][4])
                        t = taps(t, near, far, 4.0)
                        for r in (0, rows + 8) if g == groups else (8 + 8 * g,):
                            smooth[p, r : r + 8, j * LANES : (j + 1) * LANES] = t
                return c

            lax.fori_loop(0, depth + 2, xy_body, 0)

        for spacing in range(1, DMAX + 1):
            pl.when(d == spacing)(functools.partial(xy_pass, spacing))

        first, last = lane == 0, lane == LANES - 1

        def hess_body(z, c):
            def prepare(j):
                def at(dz, g):
                    return smooth[z + 1 + dz, 8 * g : 8 * g + 8, j * LANES : (j + 1) * LANES]

                centre = [at(0, g) for g in range(groups + 2)]
                above = [at(1, g) for g in range(groups + 2)]
                below = [at(-1, g) for g in range(groups + 2)]
                slope = [a - b for a, b in zip(above, below)]

                def beside(v, g):
                    up = pltpu.roll(jnp.where(top, v[g + 1], v[g]), 7, 0)
                    down = pltpu.roll(jnp.where(bottom, v[g - 1], v[g]), 1, 0)
                    return up, down

                results = []
                for g in range(1, groups + 1):
                    up, down = beside(centre, g)
                    slope_up, slope_down = beside(slope, g)
                    twice = centre[g] + centre[g]
                    hzz = (above[g] + below[g]) - twice
                    hyy = (up + down) - twice
                    zy = slope_up - slope_down
                    shifted = [
                        (pltpu.roll(v, LANES - 1, 1), pltpu.roll(v, 1, 1))
                        for v in (centre[g], slope[g], up - down)
                    ]
                    results.append((twice, hzz, hyy, zy, shifted))
                return results

            def finish(j, r, low, mid, high):
                twice, hzz, hyy, zy, shifted = mid
                plus = [jnp.where(last, high[4][i][0], shifted[i][0]) for i in range(3)]
                minus = [jnp.where(first, low[4][i][1], shifted[i][1]) for i in range(3)]
                hxx = (plus[0] + minus[0]) - twice
                zx = plus[1] - minus[1]
                yx = plus[2] - minus[2]
                flat = hxx + hyy
                trace = flat + hzz
                squares = 0.0625 * (zy * zy + zx * zx + yx * yx)
                minors = hxx * hyy + flat * hzz - squares
                value = (trace * trace * (1.0 / 3.0) - minors) * (0.5 - 0.5 * jnp.tanh(0.5 * trace))
                lanes = slice((j - 1) * LANES, j * LANES)
                resp[z, r : r + 8, lanes] = jnp.maximum(resp[z, r : r + 8, lanes], value)
                feature[pl.ds(pl.multiple_of(z * rows + r, 8), 8), lanes] = value

            ready = [prepare(0), prepare(1)]
            for j in range(1, tiles - 1):
                ready.append(prepare(j + 1))
                for g in range(groups):
                    finish(j, 8 * g, *[ready[j + i][g] for i in (-1, 0, 1)])
            return c

        lax.fori_loop(0, depth, hess_body, 0)

        xcell = xcell_ref[...]
        slots = xcell.shape[0]
        chunk = 256

        def gather_body(i, acc):
            x0 = pl.multiple_of(i * chunk, chunk)
            block = feature[:, pl.ds(x0, chunk)]
            high = block.astype(jnp.bfloat16)
            rest = (block - high.astype(jnp.float32)).astype(jnp.bfloat16)
            block = jnp.concatenate([high, rest, high], axis=0)
            where = lax.broadcasted_iota(jnp.int32, (slots, chunk), 1) + x0
            where = where + (first_tile + 1) * LANES
            where = jnp.where(where >= width, where - width, where)
            picked = jnp.dot(chosen[...], block, preferred_element_type=jnp.float32)
            kept_cells = 0.0
            for dx in range(2):
                cell = xcell + dx
                cell = jnp.where(cell == width, 0, cell)
                corner = picked[dx * slots : (dx + 1) * slots]
                kept_cells = kept_cells + jnp.where(where == cell, corner, 0.0)
            acc = acc + jnp.sum(kept_cells, axis=1, keepdims=True)
            return acc

        partial = lax.fori_loop(0, kept // chunk, gather_body, jnp.zeros((slots, 1), jnp.float32))
        column = lax.broadcasted_iota(jnp.int32, (slots, cat_ref.shape[2]), 1)
        spread = jnp.where(column == column_ref[...], partial, 0.0)
        cat_ref[level] = jnp.sum(spread, axis=0, keepdims=True)
        return carry

    lax.fori_loop(0, SCALES, level_body, 0)

    until = min(kept, width - (first_tile + 1) * LANES)
    outs = [(0, (first_tile + 1) * LANES, until)]
    if until < kept:
        outs.append((until, 0, kept - until))
    copies = [
        pltpu.make_async_copy(
            resp.at[:, :, pl.ds(low, size)], out_ref.at[:, :, pl.ds(to, size)], sems.at[n]
        )
        for n, (low, to, size) in enumerate(outs)
    ]
    for copy in copies:
        copy.start()
    for copy in copies:
        copy.wait()


def ring(axis, step):
    count = lax.axis_size(axis)
    return [(i, (i + step) % count) for i in range(count)]


def per_device(density, dilations, owner_rank, owner_slot, base_cell, corner_weights):
    depth, rows, width = density.shape
    groups = lax.axis_size("gy")

    half = width * 5 // 8 // LANES * LANES

    def z_sides(block):
        low = lax.ppermute(block[depth - HALO :], "gz", ring("gz", 1))
        high = lax.ppermute(block[:HALO], "gz", ring("gz", -1))
        return low, high

    def y_sides(block):
        sides = [lax.ppermute(block, "gy", ring("gy", 1))]
        if groups != 2:
            sides.append(lax.ppermute(block, "gy", ring("gy", -1)))
        return sides

    front = density[:, :, :half]
    beside = y_sides(front)
    low, high = z_sides(front)
    beside, back = lax.optimization_barrier((beside, density[:, :, half:]))
    parts_a = [low, density, high]
    beside_b = y_sides(back)
    for band in beside:
        low, high = z_sides(band)
        parts_a += [low, band, high]
    beside_b, parts_a = lax.optimization_barrier((beside_b, parts_a))
    low, high = z_sides(jnp.concatenate([back] + beside_b, axis=1))
    parts_b = [low, density, high]
    for band in beside_b:
        parts_b += [low, band, high]
    bands = 1 + len(beside)

    plane = (rows - 1) * width
    z_index = base_cell // plane
    remainder = base_cell % plane
    y_index = remainder // width
    x_index = remainder % width
    row_at = jnp.arange(depth * rows, dtype=jnp.int32)[None, :]
    select = []
    for step_x in (0, 1):
        chosen = 0.0
        for step_z in (0, 1):
            for step_y in (0, 1):
                row = (z_index + step_z) * rows + y_index + step_y
                weight = corner_weights[4 * step_z + 2 * step_y + step_x]
                chosen = chosen + jnp.where(row[:, None] == row_at, weight[:, None], 0.0)
        select.append(chosen)
    select = jnp.stack(select)
    column = owner_rank * HOWN + owner_slot[:, None]

    vmem = pl.BlockSpec(memory_space=pltpu.VMEM)
    anywhere = pl.BlockSpec(memory_space=pl.ANY)
    half_tiles = half // LANES
    rest_tiles = width // LANES - half_tiles

    def run(tiles, first_tile, pieces, parts, onto):
        cells = depth * rows * tiles * LANES
        operands = [dilations, select, x_index[:, None], column] + parts
        in_specs = [pl.BlockSpec(memory_space=pltpu.SMEM), vmem, vmem, vmem]
        in_specs += [anywhere] * len(parts)
        aliases = {}
        if onto is not None:
            aliases = {len(operands): 0}
            operands.append(onto)
            in_specs.append(anywhere)
        return pl.pallas_call(
            functools.partial(
                kernel, depth, rows, bands, tiles, first_tile, width, pieces, onto is not None
            ),
            out_shape=(
                jax.ShapeDtypeStruct((depth, rows, width), jnp.float32),
                jax.ShapeDtypeStruct((SCALES, 1, groups * HOWN), jnp.float32),
            ),
            in_specs=in_specs,
            out_specs=(anywhere, vmem),
            input_output_aliases=aliases,
            scratch_shapes=[
                pltpu.VMEM((depth + 2 * HALO, bands * rows, tiles * LANES), jnp.float32),
                pltpu.VMEM((depth + 2, 3 * rows, tiles * LANES), jnp.float32),
                pltpu.VMEM((depth + 2, rows + 16, tiles * LANES), jnp.float32),
                pltpu.VMEM((depth * rows, (tiles - 2) * LANES), jnp.float32),
                pltpu.VMEM((2 * base_cell.shape[0], 3 * depth * rows), jnp.bfloat16),
                pltpu.VMEM((depth, rows, (tiles - 2) * LANES), jnp.float32),
                pltpu.SemaphoreType.DMA((len(parts),)),
            ],
            compiler_params=pltpu.CompilerParams(vmem_limit_bytes=48 * 1024 * 1024),
            cost_estimate=pl.CostEstimate(
                flops=cells * SCALES * 100,
                bytes_accessed=cells * 4 * 8,
                transcendentals=cells * SCALES,
            ),
        )(*operands)

    edge = 2 * LANES
    pieces_a = (((0, 0), half, 0),)
    pieces_b = (
        ((half - edge, half - edge), edge, 0),
        ((0, half), width - half, edge),
        ((0, 0), edge, edge + width - half),
    )
    response, spread_a = run(half_tiles, 0, pieces_a, parts_a, None)
    response, spread_b = run(
        rest_tiles + 4, half_tiles - 2, pieces_b, parts_a + parts_b + parts_a, response
    )
    spread = spread_a + spread_b

    spread = spread[:, 0]
    me = lax.axis_index("gy")

    def share(owner):
        return lax.dynamic_slice_in_dim(spread, owner * HOWN, HOWN, axis=1)

    catalogue = share(me)
    for step in range(1, groups):
        catalogue = catalogue + lax.ppermute(
            share((me + step) % groups), "gy", ring("gy", step)
        )
    return (response, catalogue)


def solution(mesh):
    placed = (
        P("gz", "gy", None),
        P(),
        P(("gz", "gy"), None),
        P(("gz", "gy")),
        P(("gz", "gy")),
        P(None, ("gz", "gy")),
    )
    return jax.shard_map(
        per_device,
        mesh=mesh,
        in_specs=placed,
        out_specs=(P("gz", "gy", None), P(None, ("gz", "gy"))),
        check_vma=False,
    )
```
